512 devices in a mesh: dp: 32 (over x, y, core), ctx: 16 (over z).
Axes of the slice: x: 4, y: 4, z: 16, core: 2. Of those that a mesh axis runs over, the one named last changes fastest.
Arguments:
- prompt_kv: bfloat16 [32, 2048, 256], P('dp', 'ctx'), may hold values from -6 to 6
- queries: bfloat16 [32, 2048, 1024], P('dp', 'ctx'), may hold values from -9 to 9
- branch_kv: bfloat16 [32, 2048, 256], P('dp', 'ctx'), may hold values from -6 to 6
- dout: bfloat16 [32, 2048, 1024], P('dp', 'ctx'), may hold values from -6 to 6
- prefix: int32 [32, 32], P('dp'), may hold values from 1 to 16
Outputs:
- query_grad: bfloat16 [32, 2048, 1024], P('dp', 'ctx')
- prompt_kv_grad: bfloat16 [32, 2048, 256], P('dp', 'ctx')
- branch_kv_grad: bfloat16 [32, 2048, 256], P('dp', 'ctx')
- bias_grad: float32 [1280], replicated
The draws below stay inside these ranges and needn't reach their ends.
Inputs may be any that keep to these rules, and one draw needn't show every extreme that they name: Branch b of group g consists of rows b * 64 to b * 64 + 63 and sees prompt positions below prefix * 128.
All inputs are finite; a program needn't handle non-finite values.
Results may differ from the reference program's by a relative error of at most 0.0063.
Values may be sent and summed in bfloat16 or wider, within the bound.
No kernel may reach another device: no remote copies, remote signals or barrier semaphores. Data moves between devices by JAX's collectives and lax.ppermute only.
A program may use at most 64 MiB of HBM per device.

```python
import jax
import jax.numpy as jnp
from jax import lax

HD = 128
QH = 8
BLK = 64
KBLK = 128
P_SIZE = 2048
RB = 2048
NB = 32
N_DP = 32


def draw_prompt_kv(key, part):
    key = jax.random.fold_in(key, 7)
    shape = (N_DP, P_SIZE, 2 * HD)
    values = jnp.clip(jax.random.normal(key, shape, jnp.float32), -6.0, 6.0)
    return values.astype(jnp.bfloat16)


def draw_queries(key, part):
    key = jax.random.fold_in(key, 13)
    shape = (N_DP, RB, QH * HD)
    values = jnp.clip(jax.random.normal(key, shape, jnp.float32), -6.0, 6.0)
    return values.astype(jnp.bfloat16)


def set_ends(array, key, least, top_value):
    index_at = [jax.random.randint(jax.random.fold_in(key, axis), (), 0, length) for axis, length in enumerate(array.shape)]
    longest = array.shape.index(max(array.shape))
    next_to = index_at[:longest] + [(index_at[longest] + 1) % array.shape[longest]] + index_at[longest + 1:]
    return array.at[tuple(index_at)].set(least).at[tuple(next_to)].set(top_value)


def block_levels(rng, extent, pieces, least, high):
    gain = 1.0
    for axis_at, parts in pieces:
        heights = jax.random.uniform(jax.random.fold_in(jax.random.fold_in(rng, 6), axis_at), (parts,), jnp.float32, least / len(pieces), high / len(pieces))
        gain = gain * jnp.repeat(jnp.exp(heights), extent[axis_at] // parts).reshape((-1,) + (1,) * (len(extent) - 1 - axis_at))
    return gain


def noise(own_key, extent, width, bound, pieces=(), held_as=jnp.bfloat16):
    values = width * jax.random.normal(own_key, extent, jnp.float32)
    if pieces:
        values = values * block_levels(own_key, extent, pieces, -0.22, 0.18)
    return jnp.clip(values, -bound, bound).astype(held_as)


def setup_inputs(seed: int = 0) -> dict:
    key_of = jax.random.split(jax.random.key(seed), 6)
    return {
        "prompt_kv": draw_prompt_kv(jax.random.fold_in(key_of[5], 71), 0),
        "queries": draw_queries(jax.random.fold_in(key_of[5], 71), 0),
        "branch_kv": noise(key_of[2], (N_DP, RB, 2 * HD), 1.0, 6.0, ((0, 32), (1, 16))),
        "dout": noise(key_of[3], (N_DP, RB, QH * HD), 1.0, 6.0, ((0, 32), (1, 16))),
        "prefix": set_ends(jax.random.randint(key_of[4], (N_DP, NB), 1, P_SIZE // KBLK + 1), jax.random.fold_in(key_of[4], 1), 1, (P_SIZE // KBLK + 1) - 1).astype(jnp.int32),
    }


NEG_FILL = -1e30


def to_bf16_and_back(values):
    return lax.optimization_barrier(values.astype(jnp.bfloat16)).astype(jnp.float32)


def group_grads(prompt_rows, query_rows, branch_rows, grad_rows, prefix_row):
    score_scale = HD ** -0.5
    prompt_keys = prompt_rows[:, :HD].astype(jnp.float32)
    prompt_values = prompt_rows[:, HD:].astype(jnp.float32)
    positions = jnp.arange(P_SIZE, dtype=jnp.int32)
    within = jnp.arange(BLK, dtype=jnp.int32)
    causal = (within[None, :] <= within[:, None])[:, None, :]

    def one_block(running, inputs):
        block_q, block_do, block_kv, prefix_len = inputs
        heads_q = block_q.astype(jnp.float32).reshape(BLK, QH, HD)
        heads_do = block_do.astype(jnp.float32).reshape(BLK, QH, HD)
        own_keys = block_kv[:, :HD].astype(jnp.float32)
        own_values = block_kv[:, HD:].astype(jnp.float32)
        visible = (positions < prefix_len * KBLK)[None, None, :]
        prompt_scores = jnp.einsum("ihd,jd->ihj", heads_q, prompt_keys) * score_scale
        prompt_scores = jnp.where(visible, prompt_scores, NEG_FILL)
        own_scores = jnp.einsum("ihd,jd->ihj", heads_q, own_keys) * score_scale
        own_scores = jnp.where(causal, own_scores, NEG_FILL)
        highest = jnp.maximum(prompt_scores.max(-1), own_scores.max(-1))[..., None]
        prompt_exp = jnp.where(visible, jnp.exp(prompt_scores - highest), 0.0)
        own_exp = jnp.where(causal, jnp.exp(own_scores - highest), 0.0)
        prompt_dots = jnp.einsum("ihd,jd->ihj", heads_do, prompt_values)
        own_dots = jnp.einsum("ihd,jd->ihj", heads_do, own_values)
        total_mass = prompt_exp.sum(-1) + own_exp.sum(-1)
        log_total = highest[..., 0] + jnp.log(total_mass)
        row_delta = ((prompt_exp * prompt_dots).sum(-1) + (own_exp * own_dots).sum(-1)) / total_mass
        prompt_prob = jnp.where(visible, jnp.exp(prompt_scores - log_total[..., None]), 0.0)
        own_prob = jnp.where(causal, jnp.exp(own_scores - log_total[..., None]), 0.0)
        prompt_ds = to_bf16_and_back(prompt_prob * (prompt_dots - row_delta[..., None]))
        own_ds = to_bf16_and_back(own_prob * (own_dots - row_delta[..., None]))
        prompt_prob = to_bf16_and_back(prompt_prob)
        own_prob = to_bf16_and_back(own_prob)
        query_grad = (jnp.einsum("ihj,jd->ihd", prompt_ds, prompt_keys)
                      + jnp.einsum("ihj,jd->ihd", own_ds, own_keys)) * score_scale
        key_grad = jnp.einsum("ihj,ihd->jd", prompt_ds, heads_q) * score_scale
        value_grad = jnp.einsum("ihj,ihd->jd", prompt_prob, heads_do)
        own_key_grad = jnp.einsum("ihj,ihd->jd", own_ds, heads_q) * score_scale
        own_value_grad = jnp.einsum("ihj,ihd->jd", own_prob, heads_do)
        running = running + jnp.concatenate([key_grad, value_grad], 1)
        return running, (query_grad.reshape(BLK, QH * HD), jnp.concatenate([own_key_grad, own_value_grad], 1))

    empty_grad = jnp.zeros((P_SIZE, 2 * HD), jnp.float32)
    inputs = (query_rows.reshape(NB, BLK, QH * HD), grad_rows.reshape(NB, BLK, QH * HD),
              branch_rows.reshape(NB, BLK, 2 * HD), prefix_row)
    kv_grad, (query_grad, own_grad) = lax.scan(one_block, empty_grad, inputs)
    return kv_grad, query_grad.reshape(RB, QH * HD), own_grad.reshape(RB, 2 * HD)


def reference(prompt_kv, queries, branch_kv, dout, prefix):
    def one_group(bias_total, inputs):
        kv_grad, query_grad, own_grad = group_grads(inputs[0], inputs[1], inputs[2], inputs[3], inputs[4])
        bias_total = bias_total + jnp.concatenate([query_grad.sum(0), kv_grad.sum(0) + own_grad.sum(0)])
        return bias_total, (query_grad.astype(jnp.bfloat16), kv_grad.astype(jnp.bfloat16), own_grad.astype(jnp.bfloat16))

    bias_start = jnp.zeros((QH * HD + 2 * HD,), jnp.float32)
    bias_total, outputs = lax.scan(one_group, bias_start, (prompt_kv, queries, branch_kv, dout, prefix))
    return outputs[0], outputs[1], outputs[2], bias_total
```

```python
import functools
import math

import jax
import jax.numpy as jnp
from jax import lax
from jax.experimental import pallas as pl
from jax.experimental.pallas import tpu as pltpu
from jax.sharding import Mesh
from jax.sharding import PartitionSpec as P

BLK = 64
KBLK = 128
BP = 256
NEG = -1e30
DP = ("x", "y", "c")
CTX = ("zh", "zl")
F32 = jnp.float32
BF16 = jnp.bfloat16


def mm(a, b):
    return jnp.dot(a, b, preferred_element_type=F32)


def turn(a):
    return a.astype(F32).T.astype(BF16)


def grads_kernel(
    info, q_ref, do_ref, bkv_ref, kv_ref,
    dq_ref, bg_ref, send_ref, keep_ref, bias_ref,
    qs, dos, qt, dot_, e_s, d_s, m_s, l_s, w_s, f_s, acc,
):
    heads = q_ref.shape[1] // 128
    nb = q_ref.shape[0] // BLK
    wide = heads * BLK
    rows = nb * wide
    total = kv_ref.shape[1]
    nblk = total // BP
    scale = 128 ** -0.5
    c = scale * math.log2(math.e)
    for b in range(nb):
        for h in range(heads):
            at = (b * heads + h) * BLK
            qs[at:at + BLK, :] = q_ref[b * BLK:(b + 1) * BLK, h * 128:(h + 1) * 128]
            dos[at:at + BLK, :] = do_ref[b * BLK:(b + 1) * BLK, h * 128:(h + 1) * 128]
    qt[...] = turn(qs[...])
    dot_[...] = turn(dos[...])

    def first(blk, carry):
        at = pl.multiple_of(blk * BP, BP)
        k = kv_ref[0, pl.ds(at, BP), :]
        v = kv_ref[1, pl.ds(at, BP), :]
        pos = blk * BP + lax.broadcasted_iota(jnp.int32, (BP, wide), 0)
        for b in range(nb):
            cols = slice(b * wide, (b + 1) * wide)
            s = mm(k, qt[:, cols]) * c
            s = jnp.where(pos < info[b] * KBLK, s, NEG)
            m = s.max(0, keepdims=True)
            e = jnp.exp2(s - m)
            d = mm(v, dot_[:, cols])
            e_s[pl.ds(at, BP), cols] = e
            d_s[pl.ds(at, BP), cols] = d
            m_s[pl.ds(blk, 1), cols] = m
            l_s[pl.ds(blk, 1), cols] = e.sum(0, keepdims=True)
            w_s[pl.ds(blk, 1), cols] = (e * d).sum(0, keepdims=True)
        return carry

    lax.fori_loop(0, nblk, first, 0)

    own = []
    row_in = lax.broadcasted_iota(jnp.int32, (BLK, wide), 1) % BLK
    key_in = lax.broadcasted_iota(jnp.int32, (BLK, wide), 0)
    causal = key_in <= row_in
    for b in range(nb):
        cols = slice(b * wide, (b + 1) * wide)
        bk = bkv_ref[b * BLK:(b + 1) * BLK, :128]
        bv = bkv_ref[b * BLK:(b + 1) * BLK, 128:]
        s = jnp.where(causal, mm(bk, qt[:, cols]) * c, NEG)
        m = s.max(0, keepdims=True)
        e = jnp.exp2(s - m)
        d = mm(bv, dot_[:, cols])
        top = jnp.maximum(m, m_s[:, cols].max(0, keepdims=True))
        scales = jnp.exp2(m_s[:, cols] - top)
        mine = jnp.exp2(m - top)
        mass = (l_s[:, cols] * scales).sum(0, keepdims=True) + e.sum(0, keepdims=True) * mine
        dots = (w_s[:, cols] * scales).sum(0, keepdims=True) + (e * d).sum(0, keepdims=True) * mine
        inv = 1.0 / mass
        delta = dots * inv
        f_s[:nblk, cols] = scales * inv
        f_s[nblk:nblk + 1, cols] = delta
        p = e * (mine * inv)
        ds = (p * (d - delta)).astype(BF16)
        p = p.astype(BF16)
        own_k = mm(ds, qs[cols, :]) * scale
        own_v = mm(p, dos[cols, :])
        bg_ref[b * BLK:(b + 1) * BLK, :128] = own_k.astype(BF16)
        bg_ref[b * BLK:(b + 1) * BLK, 128:] = own_v.astype(BF16)
        own.append((own_k.sum(0, keepdims=True), own_v.sum(0, keepdims=True)))
        acc[:, cols] = mm(turn(bk), ds)

    delta = f_s[nblk:nblk + 1, :]
    even = info[nb] == 0

    def second(blk, carry):
        sum_k, sum_v = carry
        at = pl.multiple_of(blk * BP, BP)
        p = e_s[pl.ds(at, BP), :] * f_s[pl.ds(blk, 1), :]
        ds = (p * (d_s[pl.ds(at, BP), :] - delta)).astype(BF16)
        p = p.astype(BF16)
        dk = mm(ds, qs[...]) * scale
        dv = mm(p, dos[...])
        acc[...] += mm(turn(kv_ref[0, pl.ds(at, BP), :]), ds)
        keep_ref[pl.ds(at, BP), :] = jnp.where(even, dk, dv)
        send_ref[pl.ds(at, BP), :] = jnp.where(even, dv, dk).astype(BF16)
        return (sum_k + dk.sum(0, keepdims=True), sum_v + dv.sum(0, keepdims=True))

    start = (sum(o[0] for o in own), sum(o[1] for o in own))
    sum_k, sum_v = lax.fori_loop(0, nblk, second, start)
    bias_ref[...] = jnp.zeros_like(bias_ref)
    bias_ref[heads:heads + 1, :] = sum_k
    bias_ref[heads + 1:heads + 2, :] = sum_v
    dq = acc[...].T * scale
    for h in range(heads):
        part = jnp.zeros((1, 128), F32)
        for b in range(nb):
            at = (b * heads + h) * BLK
            piece = dq[at:at + BLK, :]
            part += piece.sum(0, keepdims=True)
            dq_ref[b * BLK:(b + 1) * BLK, h * 128:(h + 1) * 128] = piece.astype(BF16)
        bias_ref[h:h + 1, :] = part


def grads(info, q, do, bkv, kv):
    rows, width = q.shape
    total = kv.shape[1]
    wide = rows * width // 128
    nblk = total // BP
    vmem = pl.BlockSpec(memory_space=pltpu.VMEM)
    return pl.pallas_call(
        grads_kernel,
        out_shape=(
            jax.ShapeDtypeStruct((rows, width), BF16),
            jax.ShapeDtypeStruct((rows, 256), BF16),
            jax.ShapeDtypeStruct((total, 128), BF16),
            jax.ShapeDtypeStruct((total, 128), F32),
            jax.ShapeDtypeStruct((16, 128), F32),
        ),
        in_specs=[pl.BlockSpec(memory_space=pltpu.SMEM)] + [vmem] * 4,
        out_specs=(vmem,) * 5,
        scratch_shapes=[
            pltpu.VMEM((wide, 128), BF16),
            pltpu.VMEM((wide, 128), BF16),
            pltpu.VMEM((128, wide), BF16),
            pltpu.VMEM((128, wide), BF16),
            pltpu.VMEM((total, wide), F32),
            pltpu.VMEM((total, wide), F32),
            pltpu.VMEM((nblk, wide), F32),
            pltpu.VMEM((nblk, wide), F32),
            pltpu.VMEM((nblk, wide), F32),
            pltpu.VMEM((nblk + 8, wide), F32),
            pltpu.VMEM((128, wide), F32),
        ],
        compiler_params=pltpu.CompilerParams(vmem_limit_bytes=40 * 2**20),
        cost_estimate=pl.CostEstimate(
            flops=10 * wide * total * 128, bytes_accessed=3 * 2**20, transcendentals=wide * total
        ),
    )(info, q, do, bkv, kv)


def body(prompt_kv, queries, branch_kv, dout, prefix):
    n = lax.axis_size(CTX)
    place = lax.axis_index(CTX)
    rows = queries.shape[1]
    nb = rows // BLK
    keys = prompt_kv.shape[1]
    halves = prompt_kv[0].reshape(keys, 2, 128).transpose(1, 0, 2)
    out = jnp.broadcast_to(halves[None], (n // 2, 2, keys, 128)).reshape(n, keys, 128)
    mine = lax.all_to_all(out, CTX, 0, 0, tiled=True).reshape(1, n * keys, 128)
    kv = lax.all_gather(mine, "zl", axis=0, tiled=True)
    mine_prefix = lax.dynamic_slice_in_dim(prefix[0], place * nb, nb)
    info = jnp.concatenate([mine_prefix, lax.axis_index("zl").reshape(1)])
    dq, bg, send, keep, bias = grads(info, queries[0], dout[0], branch_kv[0], kv)
    got = lax.ppermute(send, "zl", [(0, 1), (1, 0)])
    bias = lax.psum(bias, "c")
    flat = lax.axis_size(("x", "y"))
    bias = lax.all_to_all(
        jnp.broadcast_to(bias[None], (flat, 16, 128)), ("x", "y"), 0, 0, tiled=True
    ).sum(0)
    high = bias.astype(BF16)
    low = (bias - high.astype(F32)).astype(BF16)
    extra = jnp.concatenate([high, low], 0)
    pair = (keep + got.astype(F32)).astype(BF16).reshape(n, keys, 128)
    parcel = jnp.concatenate([pair, jnp.broadcast_to(extra[None], (n, 32, 128))], 1)
    parcel = lax.all_to_all(parcel, CTX, 0, 0, tiled=True).astype(F32)
    sums = parcel.reshape(n // 2, 2, keys + 32, 128).sum(0)
    kv_grad = jnp.concatenate([sums[0, :keys], sums[1, :keys]], 1)
    bias = sums[:, keys:].sum(0)
    bias = (bias[:10] + bias[16:26]).reshape(-1)
    return dq[None], kv_grad[None].astype(BF16), bg[None], bias


def solution(mesh):
    fine = Mesh(
        mesh.devices.reshape(4, 4, 2, mesh.shape["ctx"] // 2, 2), ("x", "y", "c", "zh", "zl")
    )
    split = P(DP, CTX, None)
    return jax.shard_map(
        body,
        mesh=fine,
        in_specs=(split, split, split, split, P(DP, None)),
        out_specs=(split, split, split, P()),
        check_vma=False,
    )
```

```python
import functools
import math

import jax
import jax.numpy as jnp
from jax import lax
from jax.experimental import pallas as pl
from jax.experimental.pallas import tpu as pltpu
from jax.sharding import Mesh
from jax.sharding import PartitionSpec as P

BLK = 64
KBLK = 128
BP = 256
NEG = -1e30
DP = ("x", "y", "c")
QUAD = ("zm", "zl")
CTX = ("zh",) + QUAD
F32 = jnp.float32
BF16 = jnp.bfloat16


def mm(a, b):
    return jnp.dot(a, b, preferred_element_type=F32)


def turn(a):
    return a.astype(F32).T.astype(BF16)


def grads_kernel(
    info, q_ref, do_ref, bkv_ref, near_ref, far_ref,
    dq_ref, bg_ref, send_ref, keep_ref, bias_ref,
    qs, dos, qt, dot_, e_s, d_s, m_s, l_s, w_s, f_s, acc, kv_s,
):
    heads = q_ref.shape[1] // 128
    nb = q_ref.shape[0] // BLK
    wide = heads * BLK
    rows = nb * wide
    total = near_ref.shape[0] + far_ref.shape[0]
    nblk = total // BP
    even = info[nb] == 0
    scale = 128 ** -0.5
    c = scale * math.log2(math.e)
    for b in range(nb):
        for h in range(heads):
            at = (b * heads + h) * BLK
            qs[at:at + BLK, :] = q_ref[b * BLK:(b + 1) * BLK, h * 128:(h + 1) * 128]
            dos[at:at + BLK, :] = do_ref[b * BLK:(b + 1) * BLK, h * 128:(h + 1) * 128]
    chunk = near_ref.shape[0]
    quad = chunk // KBLK
    apart = far_ref.shape[0] // chunk
    for i in range(apart + 1):
        home = lax.rem(info[nb + 1] + i, apart + 1) * chunk
        for j in range(quad):
            at = pl.multiple_of(home + j * KBLK, KBLK)
            if i == 0:
                kv_s[pl.ds(at, KBLK), :] = near_ref[j * KBLK:(j + 1) * KBLK, :]
            else:
                src = (j * apart + i - 1) * KBLK
                kv_s[pl.ds(at, KBLK), :] = far_ref[src:src + KBLK, :]
    qt[...] = turn(qs[...])
    dot_[...] = turn(dos[...])

    def first(blk, carry):
        at = pl.multiple_of(blk * BP, BP)
        k = kv_s[pl.ds(at, BP), :128]
        v = kv_s[pl.ds(at, BP), 128:]
        pos = blk * BP + lax.broadcasted_iota(jnp.int32, (BP, wide), 0)
        for b in range(nb):
            cols = slice(b * wide, (b + 1) * wide)
            s = mm(k, qt[:, cols]) * c
            s = jnp.where(pos < info[b] * KBLK, s, NEG)
            m = s.max(0, keepdims=True)
            e = jnp.exp2(s - m)
            d = mm(v, dot_[:, cols])
            e_s[pl.ds(at, BP), cols] = e
            d_s[pl.ds(at, BP), cols] = d
            m_s[pl.ds(blk, 1), cols] = m
            l_s[pl.ds(blk, 1), cols] = e.sum(0, keepdims=True)
            w_s[pl.ds(blk, 1), cols] = (e * d).sum(0, keepdims=True)
        return carry

    lax.fori_loop(0, nblk, first, 0)

    own = []
    row_in = lax.broadcasted_iota(jnp.int32, (BLK, wide), 1) % BLK
    key_in = lax.broadcasted_iota(jnp.int32, (BLK, wide), 0)
    causal = key_in <= row_in
    for b in range(nb):
        cols = slice(b * wide, (b + 1) * wide)
        bk = bkv_ref[b * BLK:(b + 1) * BLK, :128]
        bv = bkv_ref[b * BLK:(b + 1) * BLK, 128:]
        s = jnp.where(causal, mm(bk, qt[:, cols]) * c, NEG)
        m = s.max(0, keepdims=True)
        e = jnp.exp2(s - m)
        d = mm(bv, dot_[:, cols])
        top = jnp.maximum(m, m_s[:, cols].max(0, keepdims=True))
        scales = jnp.exp2(m_s[:, cols] - top)
        mine = jnp.exp2(m - top)
        mass = (l_s[:, cols] * scales).sum(0, keepdims=True) + e.sum(0, keepdims=True) * mine
        dots = (w_s[:, cols] * scales).sum(0, keepdims=True) + (e * d).sum(0, keepdims=True) * mine
        inv = 1.0 / mass
        delta = dots * inv
        f_s[:nblk, cols] = scales * inv
        f_s[nblk:nblk + 1, cols] = delta
        p = e * (mine * inv)
        ds = (p * (d - delta)).astype(BF16)
        p = p.astype(BF16)
        own_k = mm(ds, qs[cols, :]) * scale
        own_v = mm(p, dos[cols, :])
        bg_ref[b * BLK:(b + 1) * BLK, :128] = own_k.astype(BF16)
        bg_ref[b * BLK:(b + 1) * BLK, 128:] = own_v.astype(BF16)
        own.append((own_k.sum(0, keepdims=True), own_v.sum(0, keepdims=True)))
        acc[:, cols] = mm(turn(bk), ds)

    delta = f_s[nblk:nblk + 1, :]

    def second(blk, carry):
        sum_k, sum_v = carry
        at = pl.multiple_of(blk * BP, BP)
        p = e_s[pl.ds(at, BP), :] * f_s[pl.ds(blk, 1), :]
        ds = (p * (d_s[pl.ds(at, BP), :] - delta)).astype(BF16)
        p = p.astype(BF16)
        dk = mm(ds, qs[...]) * scale
        dv = mm(p, dos[...])
        acc[...] += mm(turn(kv_s[pl.ds(at, BP), :128]), ds)
        to = pl.multiple_of(blk * KBLK, KBLK)
        for x, cols in ((dk, slice(0, 128)), (dv, slice(128, 256))):
            keep_ref[pl.ds(to, KBLK), cols] = jnp.where(even, x[:KBLK], x[KBLK:])
            send_ref[pl.ds(to, KBLK), cols] = jnp.where(even, x[KBLK:], x[:KBLK]).astype(BF16)
        return (sum_k + dk.sum(0, keepdims=True), sum_v + dv.sum(0, keepdims=True))

    start = (sum(o[0] for o in own), sum(o[1] for o in own))
    sum_k, sum_v = lax.fori_loop(0, nblk, second, start)
    bias_ref[...] = jnp.zeros_like(bias_ref)
    bias_ref[heads:heads + 1, :] = sum_k
    bias_ref[heads + 1:heads + 2, :] = sum_v
    dq = acc[...].T * scale
    for h in range(heads):
        part = jnp.zeros((1, 128), F32)
        for b in range(nb):
            at = (b * heads + h) * BLK
            piece = dq[at:at + BLK, :]
            part += piece.sum(0, keepdims=True)
            dq_ref[b * BLK:(b + 1) * BLK, h * 128:(h + 1) * 128] = piece.astype(BF16)
        bias_ref[h:h + 1, :] = part


def grads(info, q, do, bkv, near, far):
    rows, width = q.shape
    total = near.shape[0] + far.shape[0]
    wide = rows * width // 128
    nblk = total // BP
    vmem = pl.BlockSpec(memory_space=pltpu.VMEM)
    return pl.pallas_call(
        grads_kernel,
        out_shape=(
            jax.ShapeDtypeStruct((rows, width), BF16),
            jax.ShapeDtypeStruct((rows, 256), BF16),
            jax.ShapeDtypeStruct((total // 2, 256), BF16),
            jax.ShapeDtypeStruct((total // 2, 256), F32),
            jax.ShapeDtypeStruct((16, 128), F32),
        ),
        in_specs=[pl.BlockSpec(memory_space=pltpu.SMEM)] + [vmem] * 5,
        out_specs=(vmem,) * 5,
        scratch_shapes=[
            pltpu.VMEM((wide, 128), BF16),
            pltpu.VMEM((wide, 128), BF16),
            pltpu.VMEM((128, wide), BF16),
            pltpu.VMEM((128, wide), BF16),
            pltpu.VMEM((total, wide), F32),
            pltpu.VMEM((total, wide), F32),
            pltpu.VMEM((nblk, wide), F32),
            pltpu.VMEM((nblk, wide), F32),
            pltpu.VMEM((nblk, wide), F32),
            pltpu.VMEM((nblk + 8, wide), F32),
            pltpu.VMEM((128, wide), F32),
            pltpu.VMEM((total, 256), BF16),
        ],
        compiler_params=pltpu.CompilerParams(vmem_limit_bytes=40 * 2**20),
        cost_estimate=pl.CostEstimate(
            flops=10 * wide * total * 128, bytes_accessed=3 * 2**20, transcendentals=wide * total
        ),
    )(info, q, do, bkv, near, far)


SWAP = [(0, 1), (1, 0)]


def body(prompt_kv, queries, branch_kv, dout, prefix):
    n = lax.axis_size("zh")
    zh, zm, zl = (lax.axis_index(a) for a in CTX)
    rows = queries.shape[1]
    nb = rows // BLK
    keys = prompt_kv.shape[1]
    mine = prompt_kv[0]
    near = lax.all_to_all(jnp.broadcast_to(mine[None], (4, keys, 256)), QUAD, 0, 0, tiled=True)
    column = lax.all_gather(mine, "zh")
    others = lax.dynamic_slice_in_dim(jnp.concatenate([column, column]), zh + 1, n - 1)
    far = lax.all_gather(others.reshape(-1, 256), QUAD, axis=0, tiled=True)
    mine_prefix = lax.dynamic_slice_in_dim(prefix[0], lax.axis_index(CTX) * nb, nb)
    info = jnp.concatenate([mine_prefix, jnp.stack([zl, zh])])
    dq, bg, send, keep, bias = grads(
        info, queries[0], dout[0], branch_kv[0], near.reshape(-1, 256), far
    )
    got = lax.ppermute(send, "zl", SWAP)
    bias = lax.psum(bias, "c")
    flat = lax.axis_size(("x", "y"))
    bias = lax.all_to_all(
        jnp.broadcast_to(bias[None], (flat, 16, 128)), ("x", "y"), 0, 0, tiled=True
    ).sum(0)
    pair = (keep + got.astype(F32)).reshape(n, 2, keys, 256)
    away = lax.dynamic_index_in_dim(pair, 1 - zm, 1, keepdims=False).astype(BF16)
    home = lax.dynamic_index_in_dim(pair, zm, 1, keepdims=False)
    away, bias = lax.optimization_barrier((away, bias))
    got = lax.ppermute(away, "zm", SWAP)
    bias = lax.psum(bias, QUAD)
    high = bias.astype(BF16)
    low = (bias - high.astype(F32)).astype(BF16)
    extra = jnp.concatenate([high, low], 1)
    parcel = (home + got.astype(F32)).astype(BF16)
    parcel = jnp.concatenate([parcel, jnp.broadcast_to(extra[None], (n, 16, 256))], 1)
    sums = lax.all_to_all(parcel, "zh", 0, 0, tiled=True).astype(F32).sum(0)
    bias = (sums[keys:, :128] + sums[keys:, 128:])[:10].reshape(-1)
    return dq[None], sums[None, :keys].astype(BF16), bg[None], bias


def solution(mesh):
    fine = Mesh(
        mesh.devices.reshape(4, 4, 2, mesh.shape["ctx"] // 4, 2, 2),
        ("x", "y", "c", "zh", "zm", "zl"),
    )
    split = P(DP, CTX, None)
    return jax.shard_map(
        body,
        mesh=fine,
        in_specs=(split, split, split, split, P(DP, None)),
        out_specs=(split, split, split, P()),
        check_vma=False,
    )
```

```python
import functools
import math

import jax
import jax.numpy as jnp
from jax import lax
from jax.experimental import pallas as pl
from jax.experimental.pallas import tpu as pltpu
from jax.sharding import Mesh
from jax.sharding import PartitionSpec as P

BLK = 64
KBLK = 128
BP = 512
NEG = -1e30
DP = ("x", "y", "c")
QUAD = ("zm", "zl")
CTX = ("zh",) + QUAD
F32 = jnp.float32
BF16 = jnp.bfloat16


def mm(a, b):
    return jnp.dot(a, b, preferred_element_type=F32)


def nt(a, b):
    return lax.dot_general(a, b, (((1,), (1,)), ((), ())), preferred_element_type=F32)


def turn(a):
    return a.astype(F32).T.astype(BF16)


def grads_kernel(
    info, q_ref, do_ref, bkv_ref, near_ref, far_ref,
    dq_ref, bg_ref, send_ref, keep_ref, bias_ref,
    qs, dos, e_s, d_s, m_s, l_s, w_s, f_s, acc, kv_s,
):
    heads = q_ref.shape[1] // 128
    nb = q_ref.shape[0] // BLK
    wide = heads * BLK
    rows = nb * wide
    total = near_ref.shape[0] + far_ref.shape[0]
    nblk = total // BP
    units = total // KBLK
    even = info[nb] == 0
    scale = 128 ** -0.5
    c = scale * math.log2(math.e)
    for b in range(nb):
        for h in range(heads):
            at = (b * heads + h) * BLK
            qs[at:at + BLK, :] = q_ref[b * BLK:(b + 1) * BLK, h * 128:(h + 1) * 128]
            dos[at:at + BLK, :] = do_ref[b * BLK:(b + 1) * BLK, h * 128:(h + 1) * 128]
    chunk = near_ref.shape[0]
    quad = chunk // KBLK
    apart = far_ref.shape[0] // chunk
    for i in range(apart + 1):
        home = lax.rem(info[nb + 1] + i, apart + 1) * chunk
        for j in range(quad):
            at = pl.multiple_of(home + j * KBLK, KBLK)
            if i == 0:
                kv_s[pl.ds(at, KBLK), :] = near_ref[j * KBLK:(j + 1) * KBLK, :]
            else:
                src = (j * apart + i - 1) * KBLK
                kv_s[pl.ds(at, KBLK), :] = far_ref[src:src + KBLK, :]

    def first(blk, carry):
        at = pl.multiple_of(blk * BP, BP)
        k = kv_s[pl.ds(at, BP), :128]
        v = kv_s[pl.ds(at, BP), 128:]
        for b in range(nb):
            cols = slice(b * wide, (b + 1) * wide)
            s = nt(k, qs[cols, :])
            d = nt(v, dos[cols, :])
            d_s[pl.ds(at, BP), cols] = d
            for u in range(BP // KBLK):
                unit = blk * (BP // KBLK) + u
                su, du = s[u * KBLK:(u + 1) * KBLK], d[u * KBLK:(u + 1) * KBLK]
                m = su.max(0, keepdims=True)
                e = jnp.exp2((su - m) * c)
                e_s[pl.ds(at + u * KBLK, KBLK), cols] = e
                m_s[pl.ds(unit, 1), cols] = jnp.where(unit < info[b], m * c, NEG)
                l_s[pl.ds(unit, 1), cols] = e.sum(0, keepdims=True)
                w_s[pl.ds(unit, 1), cols] = (e * du).sum(0, keepdims=True)
        return carry

    lax.fori_loop(0, nblk, first, 0, unroll=4)

    own = []
    row_in = lax.broadcasted_iota(jnp.int32, (BLK, wide), 1) % BLK
    key_in = lax.broadcasted_iota(jnp.int32, (BLK, wide), 0)
    causal = key_in <= row_in
    for b in range(nb):
        cols = slice(b * wide, (b + 1) * wide)
        bk = bkv_ref[b * BLK:(b + 1) * BLK, :128]
        bv = bkv_ref[b * BLK:(b + 1) * BLK, 128:]
        s = jnp.where(causal, nt(bk, qs[cols, :]) * c, NEG)
        m = s.max(0, keepdims=True)
        e = jnp.exp2(s - m)
        d = nt(bv, dos[cols, :])
        top = jnp.maximum(m, m_s[:, cols].max(0, keepdims=True))
        scales = jnp.exp2(m_s[:, cols] - top)
        mine = jnp.exp2(m - top)
        mass = (l_s[:, cols] * scales).sum(0, keepdims=True) + e.sum(0, keepdims=True) * mine
        dots = (w_s[:, cols] * scales).sum(0, keepdims=True) + (e * d).sum(0, keepdims=True) * mine
        inv = 1.0 / mass
        delta = dots * inv
        f_s[:units, cols] = scales * inv
        f_s[units:units + 1, cols] = delta
        p = e * (mine * inv)
        ds = (p * (d - delta)).astype(BF16)
        p = p.astype(BF16)
        own_k = mm(ds, qs[cols, :]) * scale
        own_v = mm(p, dos[cols, :])
        bg_ref[b * BLK:(b + 1) * BLK, :128] = own_k.astype(BF16)
        bg_ref[b * BLK:(b + 1) * BLK, 128:] = own_v.astype(BF16)
        own.append((own_k.sum(0, keepdims=True), own_v.sum(0, keepdims=True)))
        acc[:, cols] = mm(turn(bk), ds)

    delta = f_s[units:units + 1, :]

    def second(blk, carry):
        sum_k, sum_v = carry
        at = pl.multiple_of(blk * BP, BP)
        p = jnp.concatenate([
            e_s[pl.ds(at + u * KBLK, KBLK), :] * f_s[pl.ds(blk * (BP // KBLK) + u, 1), :]
            for u in range(BP // KBLK)
        ])
        ds = (p * (d_s[pl.ds(at, BP), :] - delta)).astype(BF16)
        p = p.astype(BF16)
        dk = mm(ds, qs[...]) * scale
        dv = mm(p, dos[...])
        acc[...] += mm(turn(kv_s[pl.ds(at, BP), :128]), ds)
        for u in range(0, BP // KBLK, 2):
            to = pl.multiple_of(blk * (BP // 2) + u * (KBLK // 2), KBLK)
            for x, cols in ((dk, slice(0, 128)), (dv, slice(128, 256))):
                x0, x1 = x[u * KBLK:(u + 1) * KBLK], x[(u + 1) * KBLK:(u + 2) * KBLK]
                keep_ref[pl.ds(to, KBLK), cols] = jnp.where(even, x0, x1)
                send_ref[pl.ds(to, KBLK), cols] = jnp.where(even, x1, x0).astype(BF16)
        return (sum_k + dk.sum(0, keepdims=True), sum_v + dv.sum(0, keepdims=True))

    start = (sum(o[0] for o in own), sum(o[1] for o in own))
    sum_k, sum_v = lax.fori_loop(0, nblk, second, start, unroll=4)
    parts = []
    dq = acc[...].T * scale
    for h in range(heads):
        part = jnp.zeros((1, 128), F32)
        for b in range(nb):
            at = (b * heads + h) * BLK
            piece = dq[at:at + BLK, :]
            part += piece.sum(0, keepdims=True)
            dq_ref[b * BLK:(b + 1) * BLK, h * 128:(h + 1) * 128] = piece.astype(BF16)
        parts.append(part)
    parts += [sum_k, sum_v, jnp.zeros((14 - heads, 128), F32)]
    bias_ref[...] = jnp.broadcast_to(jnp.concatenate(parts)[None], bias_ref.shape)


def grads(info, q, do, bkv, near, far, copies):
    rows, width = q.shape
    total = near.shape[0] + far.shape[0]
    wide = rows * width // 128
    units = total // KBLK
    vmem = pl.BlockSpec(memory_space=pltpu.VMEM)
    return pl.pallas_call(
        grads_kernel,
        out_shape=(
            jax.ShapeDtypeStruct((rows, width), BF16),
            jax.ShapeDtypeStruct((rows, 256), BF16),
            jax.ShapeDtypeStruct((total // 2, 256), BF16),
            jax.ShapeDtypeStruct((total // 2, 256), F32),
            jax.ShapeDtypeStruct((copies, 16, 128), F32),
        ),
        in_specs=[pl.BlockSpec(memory_space=pltpu.SMEM)] + [vmem] * 5,
        out_specs=(vmem,) * 5,
        scratch_shapes=[
            pltpu.VMEM((wide, 128), BF16),
            pltpu.VMEM((wide, 128), BF16),
            pltpu.VMEM((total, wide), F32),
            pltpu.VMEM((total, wide), F32),
            pltpu.VMEM((units, wide), F32),
            pltpu.VMEM((units, wide), F32),
            pltpu.VMEM((units, wide), F32),
            pltpu.VMEM((units + 8, wide), F32),
            pltpu.VMEM((128, wide), F32),
            pltpu.VMEM((total, 256), BF16),
        ],
        compiler_params=pltpu.CompilerParams(vmem_limit_bytes=40 * 2**20),
        cost_estimate=pl.CostEstimate(
            flops=10 * wide * total * 128, bytes_accessed=3 * 2**20, transcendentals=wide * total
        ),
    )(info, q, do, bkv, near, far)


SWAP = [(0, 1), (1, 0)]


def body(prompt_kv, queries, branch_kv, dout, prefix):
    n = lax.axis_size("zh")
    zh, zm, zl = (lax.axis_index(a) for a in CTX)
    rows = queries.shape[1]
    nb = rows // BLK
    keys = prompt_kv.shape[1]
    mine = prompt_kv[0]
    near = lax.all_to_all(jnp.broadcast_to(mine[None], (4, keys, 256)), QUAD, 0, 0, tiled=True)
    column = lax.all_gather(mine, "zh")
    others = lax.dynamic_slice_in_dim(jnp.concatenate([column, column]), zh + 1, n - 1)
    far = lax.all_gather(others.reshape(-1, 256), QUAD, axis=0, tiled=True)
    mine_prefix = lax.dynamic_slice_in_dim(prefix[0], lax.axis_index(CTX) * nb, nb)
    info = jnp.concatenate([mine_prefix, jnp.stack([zl, zh])])
    dq, bg, send, keep, bias = grads(
        info, queries[0], dout[0], branch_kv[0], near.reshape(-1, 256), far, lax.axis_size(DP)
    )
    got = lax.ppermute(send, "zl", SWAP)
    bias = lax.all_to_all(bias, DP, 0, 0, tiled=True)
    pair = (keep + got.astype(F32)).reshape(n, 2, keys, 256)
    away = lax.dynamic_index_in_dim(pair, 1 - zm, 1, keepdims=False).astype(BF16)
    home = lax.dynamic_index_in_dim(pair, zm, 1, keepdims=False)
    got = lax.ppermute(away, "zm", SWAP)
    bias, away = lax.optimization_barrier((bias, away))
    bias = bias.sum(0)
    bias = lax.psum(bias, QUAD)
    high = bias.astype(BF16)
    low = (bias - high.astype(F32)).astype(BF16)
    extra = jnp.concatenate([high, low], 1)
    parcel = (home + got.astype(F32)).astype(BF16)
    parcel = jnp.concatenate([parcel, jnp.broadcast_to(extra[None], (n, 16, 256))], 1)
    sums = lax.all_to_all(parcel, "zh", 0, 0, tiled=True).astype(F32).sum(0)
    bias = (sums[keys:, :128] + sums[keys:, 128:])[:10].reshape(-1)
    return dq[None], sums[None, :keys].astype(BF16), bg[None], bias


def solution(mesh):
    fine = Mesh(
        mesh.devices.reshape(4, 4, 2, mesh.shape["ctx"] // 4, 2, 2),
        ("x", "y", "c", "zh", "zm", "zl"),
    )
    split = P(DP, CTX, None)
    return jax.shard_map(
        body,
        mesh=fine,
        in_specs=(split, split, split, split, P(DP, None)),
        out_specs=(split, split, split, P()),
        check_vma=False,
    )
```

```python
import functools
import math

import jax
import jax.numpy as jnp
from jax import lax
from jax.experimental import pallas as pl
from jax.experimental.pallas import tpu as pltpu
from jax.sharding import Mesh
from jax.sharding import PartitionSpec as P

BLK = 64
KBLK = 128
ORDER = (2, 1, 3)
BP = 512
NEG = -1e30
DP = ("x", "y", "c")
QUAD = ("zm", "zl")
CTX = ("zh",) + QUAD
F32 = jnp.float32
BF16 = jnp.bfloat16


def mm(a, b):
    return jnp.dot(a, b, preferred_element_type=F32)


def nt(a, b):
    return lax.dot_general(a, b, (((1,), (1,)), ((), ())), preferred_element_type=F32)


def turn(a):
    return a.astype(F32).T.astype(BF16)


def grads_kernel(
    info, q_ref, do_ref, bkv_ref, near_ref, far_ref,
    dq_ref, bg_ref, send_ref, keep_ref, bias_ref,
    qs, dos, e_s, d_s, m_s, l_s, w_s, f_s, acc, kv_s,
):
    heads = q_ref.shape[1] // 128
    nb = q_ref.shape[0] // BLK
    wide = heads * BLK
    rows = nb * wide
    total = near_ref.shape[0] + far_ref.shape[0]
    nblk = total // BP
    units = total // KBLK
    even = info[nb] == 0
    scale = 128 ** -0.5
    c = scale * math.log2(math.e)
    for b in range(nb):
        for h in range(heads):
            at = (b * heads + h) * BLK
            qs[at:at + BLK, :] = q_ref[b * BLK:(b + 1) * BLK, h * 128:(h + 1) * 128]
            dos[at:at + BLK, :] = do_ref[b * BLK:(b + 1) * BLK, h * 128:(h + 1) * 128]
    chunk = near_ref.shape[0]
    quad = chunk // KBLK
    apart = far_ref.shape[0] // chunk
    for i in range(apart + 1):
        home = lax.rem(info[nb + 1] + i, apart + 1) * chunk
        for j in range(quad):
            at = pl.multiple_of(home + j * KBLK, KBLK)
            if i == 0:
                kv_s[pl.ds(at, KBLK), :] = near_ref[j * KBLK:(j + 1) * KBLK, :]
            else:
                src = (j * apart + i - 1) * KBLK
                kv_s[pl.ds(at, KBLK), :] = far_ref[src:src + KBLK, :]

    def first(blk, carry):
        at = pl.multiple_of(blk * BP, BP)
        k = kv_s[pl.ds(at, BP), :128]
        v = kv_s[pl.ds(at, BP), 128:]
        for b in range(nb):
            cols = slice(b * wide, (b + 1) * wide)
            s = nt(k, qs[cols, :])
            d = nt(v, dos[cols, :])
            d_s[pl.ds(at, BP), cols] = d
            for u in range(BP // KBLK):
                unit = blk * (BP // KBLK) + u
                su, du = s[u * KBLK:(u + 1) * KBLK], d[u * KBLK:(u + 1) * KBLK]
                m = su.max(0, keepdims=True)
                e = jnp.exp2((su - m) * c)
                e_s[pl.ds(at + u * KBLK, KBLK), cols] = e
                m_s[pl.ds(unit, 1), cols] = jnp.where(unit < info[b], m * c, NEG)
                l_s[pl.ds(unit, 1), cols] = e.sum(0, keepdims=True)
                w_s[pl.ds(unit, 1), cols] = (e * du).sum(0, keepdims=True)
        return carry

    lax.fori_loop(0, nblk, first, 0, unroll=4)

    own = []
    row_in = lax.broadcasted_iota(jnp.int32, (BLK, wide), 1) % BLK
    key_in = lax.broadcasted_iota(jnp.int32, (BLK, wide), 0)
    causal = key_in <= row_in
    for b in range(nb):
        cols = slice(b * wide, (b + 1) * wide)
        bk = bkv_ref[b * BLK:(b + 1) * BLK, :128]
        bv = bkv_ref[b * BLK:(b + 1) * BLK, 128:]
        s = jnp.where(causal, nt(bk, qs[cols, :]) * c, NEG)
        m = s.max(0, keepdims=True)
        e = jnp.exp2(s - m)
        d = nt(bv, dos[cols, :])
        top = jnp.maximum(m, m_s[:, cols].max(0, keepdims=True))
        scales = jnp.exp2(m_s[:, cols] - top)
        mine = jnp.exp2(m - top)
        mass = (l_s[:, cols] * scales).sum(0, keepdims=True) + e.sum(0, keepdims=True) * mine
        dots = (w_s[:, cols] * scales).sum(0, keepdims=True) + (e * d).sum(0, keepdims=True) * mine
        inv = 1.0 / mass
        delta = dots * inv
        f_s[:units, cols] = scales * inv
        f_s[units:units + 1, cols] = delta
        p = e * (mine * inv)
        ds = (p * (d - delta)).astype(BF16)
        p = p.astype(BF16)
        own_k = mm(ds, qs[cols, :]) * scale
        own_v = mm(p, dos[cols, :])
        bg_ref[b * BLK:(b + 1) * BLK, :128] = own_k.astype(BF16)
        bg_ref[b * BLK:(b + 1) * BLK, 128:] = own_v.astype(BF16)
        own.append((own_k.sum(0, keepdims=True), own_v.sum(0, keepdims=True)))
        acc[:, cols] = mm(turn(bk), ds)

    delta = f_s[units:units + 1, :]

    def second(blk, carry):
        sum_k, sum_v = carry
        at = pl.multiple_of(blk * BP, BP)
        p = jnp.concatenate([
            e_s[pl.ds(at + u * KBLK, KBLK), :] * f_s[pl.ds(blk * (BP // KBLK) + u, 1), :]
            for u in range(BP // KBLK)
        ])
        ds = (p * (d_s[pl.ds(at, BP), :] - delta)).astype(BF16)
        p = p.astype(BF16)
        dk = mm(ds, qs[...]) * scale
        dv = mm(p, dos[...])
        acc[...] += mm(turn(kv_s[pl.ds(at, BP), :128]), ds)
        for u in range(0, BP // KBLK, 2):
            to = pl.multiple_of(blk * (BP // 2) + u * (KBLK // 2), KBLK)
            for x, cols in ((dk, slice(0, 128)), (dv, slice(128, 256))):
                x0, x1 = x[u * KBLK:(u + 1) * KBLK], x[(u + 1) * KBLK:(u + 2) * KBLK]
                keep_ref[pl.ds(to, KBLK), cols] = jnp.where(even, x0, x1)
                send_ref[pl.ds(to, KBLK), cols] = jnp.where(even, x1, x0).astype(BF16)
        return (sum_k + dk.sum(0, keepdims=True), sum_v + dv.sum(0, keepdims=True))

    start = (sum(o[0] for o in own), sum(o[1] for o in own))
    sum_k, sum_v = lax.fori_loop(0, nblk, second, start, unroll=4)
    parts = []
    dq = acc[...].T * scale
    for h in range(heads):
        part = jnp.zeros((1, 128), F32)
        for b in range(nb):
            at = (b * heads + h) * BLK
            piece = dq[at:at + BLK, :]
            part += piece.sum(0, keepdims=True)
            dq_ref[b * BLK:(b + 1) * BLK, h * 128:(h + 1) * 128] = piece.astype(BF16)
        parts.append(part)
    parts += [sum_k, sum_v, jnp.zeros((14 - heads, 128), F32)]
    bias_ref[...] = jnp.broadcast_to(jnp.concatenate(parts)[None], bias_ref.shape)


def grads(info, q, do, bkv, near, far, copies):
    rows, width = q.shape
    total = near.shape[0] + far.shape[0]
    wide = rows * width // 128
    units = total // KBLK
    vmem = pl.BlockSpec(memory_space=pltpu.VMEM)
    return pl.pallas_call(
        grads_kernel,
        out_shape=(
            jax.ShapeDtypeStruct((rows, width), BF16),
            jax.ShapeDtypeStruct((rows, 256), BF16),
            jax.ShapeDtypeStruct((total // 2, 256), BF16),
            jax.ShapeDtypeStruct((total // 2, 256), F32),
            jax.ShapeDtypeStruct((copies, 16, 128), F32),
        ),
        in_specs=[pl.BlockSpec(memory_space=pltpu.SMEM)] + [vmem] * 5,
        out_specs=(vmem,) * 5,
        scratch_shapes=[
            pltpu.VMEM((wide, 128), BF16),
            pltpu.VMEM((wide, 128), BF16),
            pltpu.VMEM((total, wide), F32),
            pltpu.VMEM((total, wide), F32),
            pltpu.VMEM((units, wide), F32),
            pltpu.VMEM((units, wide), F32),
            pltpu.VMEM((units, wide), F32),
            pltpu.VMEM((units + 8, wide), F32),
            pltpu.VMEM((128, wide), F32),
            pltpu.VMEM((total, 256), BF16),
        ],
        compiler_params=pltpu.CompilerParams(vmem_limit_bytes=40 * 2**20),
        cost_estimate=pl.CostEstimate(
            flops=10 * wide * total * 128, bytes_accessed=3 * 2**20, transcendentals=wide * total
        ),
    )(info, q, do, bkv, near, far)


SWAP = [(0, 1), (1, 0)]


def body(prompt_kv, queries, branch_kv, dout, prefix):
    n = lax.axis_size("zh")
    zh, zm, zl = (lax.axis_index(a) for a in CTX)
    rows = queries.shape[1]
    nb = rows // BLK
    keys = prompt_kv.shape[1]
    mine = prompt_kv[0]
    column = lax.all_gather(mine, "zh")
    mine, column = lax.optimization_barrier((mine, column))
    near = lax.all_to_all(jnp.broadcast_to(mine[None], (4, keys, 256)), QUAD, 0, 0, tiled=True)
    others = lax.dynamic_slice_in_dim(jnp.concatenate([column, column]), zh + 1, n - 1)
    far = lax.all_gather(others.reshape(-1, 256), QUAD, axis=0, tiled=True)
    mine_prefix = lax.dynamic_slice_in_dim(prefix[0], lax.axis_index(CTX) * nb, nb)
    info = jnp.concatenate([mine_prefix, jnp.stack([zl, zh])])
    dq, bg, send, keep, bias = grads(
        info, queries[0], dout[0], branch_kv[0], near.reshape(-1, 256), far, lax.axis_size(DP)
    )
    got = lax.ppermute(send, "zl", SWAP)
    bias = lax.all_to_all(bias, DP, 0, 0, tiled=True)
    pair = (keep + got.astype(F32)).reshape(n, 2, keys, 256)
    away = lax.dynamic_index_in_dim(pair, 1 - zm, 1, keepdims=False).astype(BF16)
    home = lax.dynamic_index_in_dim(pair, zm, 1, keepdims=False)
    got = lax.ppermute(away, "zm", SWAP)
    bias, away = lax.optimization_barrier((bias, away))
    bias = bias.sum(0)
    bias = lax.psum(lax.psum(bias, "zl"), "zm")
    high = bias.astype(BF16)
    low = (bias - high.astype(F32)).astype(BF16)
    extra = jnp.concatenate([high, low], 1)
    parcel = home + got.astype(F32)
    sums = lax.dynamic_index_in_dim(parcel, zh, 0, keepdims=False)
    both = jnp.zeros((16, 256), F32)
    for far in ORDER:
        sent = lax.dynamic_index_in_dim(parcel, (zh + far) % n, 0, keepdims=False)
        sent = jnp.concatenate([sent.astype(BF16), extra])
        came = lax.ppermute(sent, "zh", [(p, (p + far) % n) for p in range(n)]).astype(F32)
        sums += came[:keys]
        both += came[keys:]
    bias = (bias + both[:, :128] + both[:, 128:])[:10].reshape(-1)
    return dq[None], sums[None].astype(BF16), bg[None], bias


def solution(mesh):
    fine = Mesh(
        mesh.devices.reshape(4, 4, 2, mesh.shape["ctx"] // 4, 2, 2),
        ("x", "y", "c", "zh", "zm", "zl"),
    )
    split = P(DP, CTX, None)
    return jax.shard_map(
        body,
        mesh=fine,
        in_specs=(split, split, split, split, P(DP, None)),
        out_specs=(split, split, split, P()),
        check_vma=False,
    )
```

```python
import functools
import math

import jax
import jax.numpy as jnp
from jax import lax
from jax.experimental import pallas as pl
from jax.experimental.pallas import tpu as pltpu
from jax.sharding import Mesh
from jax.sharding import PartitionSpec as P

BLK = 64
KBLK = 128
ORDER = (2, 1, 3)
BP = 512
NEG = -1e30
DP = ("x", "y", "c")
QUAD = ("zm", "zl")
CTX = ("zh",) + QUAD
F32 = jnp.float32
BF16 = jnp.bfloat16


def mm(a, b):
    return jnp.dot(a, b, preferred_element_type=F32)


def nt(a, b):
    return lax.dot_general(a, b, (((1,), (1,)), ((), ())), preferred_element_type=F32)


def turn(a):
    return a.astype(F32).T.astype(BF16)


def grads_kernel(
    info, q_ref, do_ref, bkv_ref, near_ref, far_ref,
    dq_ref, bg_ref, send_ref, keep_ref, bias_ref,
    qs, dos, e_s, d_s, m_s, l_s, w_s, f_s, acc, kv_s,
):
    heads = q_ref.shape[1] // 128
    nb = q_ref.shape[0] // BLK
    wide = heads * BLK
    rows = nb * wide
    total = near_ref.shape[0] + far_ref.shape[0]
    nblk = total // BP
    units = total // KBLK
    even = info[nb] == 0
    scale = 128 ** -0.5
    c = scale * math.log2(math.e)
    for b in range(nb):
        for h in range(heads):
            at = (b * heads + h) * BLK
            qs[at:at + BLK, :] = q_ref[b * BLK:(b + 1) * BLK, h * 128:(h + 1) * 128]
            dos[at:at + BLK, :] = do_ref[b * BLK:(b + 1) * BLK, h * 128:(h + 1) * 128]
    chunk = near_ref.shape[0]
    quad = chunk // KBLK
    apart = far_ref.shape[0] // chunk
    for i in range(apart + 1):
        home = lax.rem(info[nb + 1] + i, apart + 1) * chunk
        for j in range(quad):
            at = pl.multiple_of(home + j * KBLK, KBLK)
            if i == 0:
                kv_s[pl.ds(at, KBLK), :] = near_ref[j * KBLK:(j + 1) * KBLK, :]
            else:
                src = (j * apart + i - 1) * KBLK
                kv_s[pl.ds(at, KBLK), :] = far_ref[src:src + KBLK, :]

    def first(blk, carry):
        at = pl.multiple_of(blk * BP, BP)
        k = kv_s[pl.ds(at, BP), :128]
        v = kv_s[pl.ds(at, BP), 128:]
        for b in range(nb):
            cols = slice(b * wide, (b + 1) * wide)
            s = nt(k, qs[cols, :])
            d = nt(v, dos[cols, :])
            d_s[pl.ds(at, BP), cols] = d
            for u in range(BP // KBLK):
                unit = blk * (BP // KBLK) + u
                su, du = s[u * KBLK:(u + 1) * KBLK], d[u * KBLK:(u + 1) * KBLK]
                m = su.max(0, keepdims=True)
                e = jnp.exp2((su - m) * c)
                e_s[pl.ds(at + u * KBLK, KBLK), cols] = e
                m_s[pl.ds(unit, 1), cols] = jnp.where(unit < info[b], m * c, NEG)
                l_s[pl.ds(unit, 1), cols] = e.sum(0, keepdims=True)
                w_s[pl.ds(unit, 1), cols] = (e * du).sum(0, keepdims=True)
        return carry

    lax.fori_loop(0, nblk, first, 0, unroll=4)

    own = []
    row_in = lax.broadcasted_iota(jnp.int32, (BLK, wide), 1) % BLK
    key_in = lax.broadcasted_iota(jnp.int32, (BLK, wide), 0)
    causal = key_in <= row_in
    for b in range(nb):
        cols = slice(b * wide, (b + 1) * wide)
        bk = bkv_ref[b * BLK:(b + 1) * BLK, :128]
        bv = bkv_ref[b * BLK:(b + 1) * BLK, 128:]
        s = jnp.where(causal, nt(bk, qs[cols, :]) * c, NEG)
        m = s.max(0, keepdims=True)
        e = jnp.exp2(s - m)
        d = nt(bv, dos[cols, :])
        top = jnp.maximum(m, m_s[:, cols].max(0, keepdims=True))
        scales = jnp.exp2(m_s[:, cols] - top)
        mine = jnp.exp2(m - top)
        mass = (l_s[:, cols] * scales).sum(0, keepdims=True) + e.sum(0, keepdims=True) * mine
        dots = (w_s[:, cols] * scales).sum(0, keepdims=True) + (e * d).sum(0, keepdims=True) * mine
        inv = 1.0 / mass
        delta = dots * inv
        f_s[:units, cols] = scales * inv
        f_s[units:units + 1, cols] = delta
        p = e * (mine * inv)
        ds = (p * (d - delta)).astype(BF16)
        p = p.astype(BF16)
        own_k = mm(ds, qs[cols, :]) * scale
        own_v = mm(p, dos[cols, :])
        bg_ref[b * BLK:(b + 1) * BLK, :128] = own_k.astype(BF16)
        bg_ref[b * BLK:(b + 1) * BLK, 128:] = own_v.astype(BF16)
        own.append((own_k.sum(0, keepdims=True), own_v.sum(0, keepdims=True)))
        acc[:, cols] = mm(turn(bk), ds)

    delta = f_s[units:units + 1, :]

    def second(blk, carry):
        sum_k, sum_v = carry
        at = pl.multiple_of(blk * BP, BP)
        p = jnp.concatenate([
            e_s[pl.ds(at + u * KBLK, KBLK), :] * f_s[pl.ds(blk * (BP // KBLK) + u, 1), :]
            for u in range(BP // KBLK)
        ])
        ds = (p * (d_s[pl.ds(at, BP), :] - delta)).astype(BF16)
        p = p.astype(BF16)
        dk = mm(ds, qs[...]) * scale
        dv = mm(p, dos[...])
        acc[...] += mm(turn(kv_s[pl.ds(at, BP), :128]), ds)
        for u in range(0, BP // KBLK, 2):
            to = pl.multiple_of(blk * (BP // 2) + u * (KBLK // 2), KBLK)
            for x, cols in ((dk, slice(0, 128)), (dv, slice(128, 256))):
                x0, x1 = x[u * KBLK:(u + 1) * KBLK], x[(u + 1) * KBLK:(u + 2) * KBLK]
                keep_ref[pl.ds(to, KBLK), cols] = jnp.where(even, x0, x1)
                send_ref[pl.ds(to, KBLK), cols] = jnp.where(even, x1, x0).astype(BF16)
        return (sum_k + dk.sum(0, keepdims=True), sum_v + dv.sum(0, keepdims=True))

    start = (sum(o[0] for o in own), sum(o[1] for o in own))
    sum_k, sum_v = lax.fori_loop(0, nblk, second, start, unroll=4)
    parts = []
    dq = acc[...].T * scale
    for h in range(heads):
        part = jnp.zeros((1, 128), F32)
        for b in range(nb):
            at = (b * heads + h) * BLK
            piece = dq[at:at + BLK, :]
            part += piece.sum(0, keepdims=True)
            dq_ref[b * BLK:(b + 1) * BLK, h * 128:(h + 1) * 128] = piece.astype(BF16)
        parts.append(part)
    parts += [sum_k, sum_v, jnp.zeros((14 - heads, 128), F32)]
    bias_ref[...] = jnp.broadcast_to(jnp.concatenate(parts)[None], bias_ref.shape)


def grads(info, q, do, bkv, near, far, copies):
    rows, width = q.shape
    total = near.shape[0] + far.shape[0]
    wide = rows * width // 128
    units = total // KBLK
    vmem = pl.BlockSpec(memory_space=pltpu.VMEM)
    return pl.pallas_call(
        grads_kernel,
        out_shape=(
            jax.ShapeDtypeStruct((rows, width), BF16),
            jax.ShapeDtypeStruct((rows, 256), BF16),
            jax.ShapeDtypeStruct((total // 2, 256), BF16),
            jax.ShapeDtypeStruct((total // 2, 256), F32),
            jax.ShapeDtypeStruct((copies, 16, 128), F32),
        ),
        in_specs=[pl.BlockSpec(memory_space=pltpu.SMEM)] + [vmem] * 5,
        out_specs=(vmem,) * 5,
        scratch_shapes=[
            pltpu.VMEM((wide, 128), BF16),
            pltpu.VMEM((wide, 128), BF16),
            pltpu.VMEM((total, wide), F32),
            pltpu.VMEM((total, wide), F32),
            pltpu.VMEM((units, wide), F32),
            pltpu.VMEM((units, wide), F32),
            pltpu.VMEM((units, wide), F32),
            pltpu.VMEM((units + 8, wide), F32),
            pltpu.VMEM((128, wide), F32),
            pltpu.VMEM((total, 256), BF16),
        ],
        compiler_params=pltpu.CompilerParams(vmem_limit_bytes=40 * 2**20),
        cost_estimate=pl.CostEstimate(
            flops=10 * wide * total * 128, bytes_accessed=3 * 2**20, transcendentals=wide * total
        ),
    )(info, q, do, bkv, near, far)


SWAP = [(0, 1), (1, 0)]


def body(prompt_kv, queries, branch_kv, dout, prefix):
    n = lax.axis_size("zh")
    zh, zm, zl = (lax.axis_index(a) for a in CTX)
    rows = queries.shape[1]
    nb = rows // BLK
    keys = prompt_kv.shape[1]
    mine = prompt_kv[0]
    column = lax.all_gather(mine, "zh")
    mine, column = lax.optimization_barrier((mine, column))
    near = lax.all_to_all(jnp.broadcast_to(mine[None], (4, keys, 256)), QUAD, 0, 0, tiled=True)
    others = lax.dynamic_slice_in_dim(jnp.concatenate([column, column]), zh + 1, n - 1)
    far = lax.all_gather(others.reshape(-1, 256), QUAD, axis=0, tiled=True)
    mine_prefix = lax.dynamic_slice_in_dim(prefix[0], lax.axis_index(CTX) * nb, nb)
    info = jnp.concatenate([mine_prefix, jnp.stack([zl, zh])])
    dq, bg, send, keep, bias = grads(
        info, queries[0], dout[0], branch_kv[0], near.reshape(-1, 256), far, lax.axis_size(DP)
    )
    got = lax.ppermute(send, "zl", SWAP)
    bias = lax.all_to_all(bias, DP, 0, 0, tiled=True)
    pair = (keep + got.astype(F32)).reshape(n, 2, keys, 256)
    away = lax.dynamic_index_in_dim(pair, 1 - zm, 1, keepdims=False).astype(BF16)
    home = lax.dynamic_index_in_dim(pair, zm, 1, keepdims=False)
    got = lax.ppermute(away, "zm", SWAP)
    bias, away = lax.optimization_barrier((bias, away))
    bias = bias.sum(0)
    bias = lax.psum(bias, QUAD)
    high = bias.astype(BF16)
    low = (bias - high.astype(F32)).astype(BF16)
    extra = jnp.concatenate([high, low], 1)
    parcel = home + got.astype(F32)
    sums = lax.dynamic_index_in_dim(parcel, zh, 0, keepdims=False)
    both = jnp.zeros((16, 256), F32)
    for far in ORDER:
        sent = lax.dynamic_index_in_dim(parcel, (zh + far) % n, 0, keepdims=False)
        sent = jnp.concatenate([sent.astype(BF16), extra])
        came = lax.ppermute(sent, "zh", [(p, (p + far) % n) for p in range(n)]).astype(F32)
        sums += came[:keys]
        both += came[keys:]
    bias = (bias + both[:, :128] + both[:, 128:])[:10].reshape(-1)
    return dq[None], sums[None].astype(BF16), bg[None], bias


def solution(mesh):
    fine = Mesh(
        mesh.devices.reshape(4, 4, 2, mesh.shape["ctx"] // 4, 2, 2),
        ("x", "y", "c", "zh", "zm", "zl"),
    )
    split = P(DP, CTX, None)
    return jax.shard_map(
        body,
        mesh=fine,
        in_specs=(split, split, split, split, P(DP, None)),
        out_specs=(split, split, split, P()),
        check_vma=False,
    )
```

```python
import functools
import math

import jax
import jax.numpy as jnp
from jax import lax
from jax.experimental import pallas as pl
from jax.experimental.pallas import tpu as pltpu
from jax.sharding import Mesh
from jax.sharding import PartitionSpec as P

BLK = 64
KBLK = 128
ORDER = (2, 1, 3)
BP = 1024
NEG = -1e30
DP = ("x", "y", "c")
QUAD = ("zm", "zl")
CTX = ("zh",) + QUAD
F32 = jnp.float32
BF16 = jnp.bfloat16


def mm(a, b):
    return jnp.dot(a, b, preferred_element_type=F32)


def nt(a, b):
    return lax.dot_general(a, b, (((1,), (1,)), ((), ())), preferred_element_type=F32)


def turn(a):
    return a.astype(F32).T.astype(BF16)


def grads_kernel(
    info, q_ref, do_ref, bkv_ref, near_ref, far_ref,
    dq_ref, bg_ref, send_ref, keep_ref, bias_ref,
    qs, dos, e_s, d_s, m_s, l_s, w_s, f_s, acc, kv_s,
):
    heads = q_ref.shape[1] // 128
    nb = q_ref.shape[0] // BLK
    wide = heads * BLK
    rows = nb * wide
    total = near_ref.shape[0] + far_ref.shape[0]
    nblk = total // BP
    units = total // KBLK
    even = info[nb] == 0
    scale = 128 ** -0.5
    c = scale * math.log2(math.e)
    for b in range(nb):
        for h in range(heads):
            at = (b * heads + h) * BLK
            qs[at:at + BLK, :] = q_ref[b * BLK:(b + 1) * BLK, h * 128:(h + 1) * 128]
            dos[at:at + BLK, :] = do_ref[b * BLK:(b + 1) * BLK, h * 128:(h + 1) * 128]
    chunk = near_ref.shape[0]
    quad = chunk // KBLK
    apart = far_ref.shape[0] // chunk
    for i in range(apart + 1):
        home = lax.rem(info[nb + 1] + i, apart + 1) * chunk
        for j in range(quad):
            at = pl.multiple_of(home + j * KBLK, KBLK)
            if i == 0:
                kv_s[pl.ds(at, KBLK), :] = near_ref[j * KBLK:(j + 1) * KBLK, :]
            else:
                src = (j * apart + i - 1) * KBLK
                kv_s[pl.ds(at, KBLK), :] = far_ref[src:src + KBLK, :]

    def first(blk, carry):
        at = pl.multiple_of(blk * BP, BP)
        k = kv_s[pl.ds(at, BP), :128]
        v = kv_s[pl.ds(at, BP), 128:]
        for b in range(nb):
            cols = slice(b * wide, (b + 1) * wide)
            s = nt(k, qs[cols, :])
            d = nt(v, dos[cols, :])
            d_s[pl.ds(at, BP), cols] = d
            for u in range(BP // KBLK):
                unit = blk * (BP // KBLK) + u
                su, du = s[u * KBLK:(u + 1) * KBLK], d[u * KBLK:(u + 1) * KBLK]
                m = su.max(0, keepdims=True)
                e = jnp.exp2((su - m) * c)
                e_s[pl.ds(at + u * KBLK, KBLK), cols] = e
                m_s[pl.ds(unit, 1), cols] = jnp.where(unit < info[b], m * c, NEG)
                l_s[pl.ds(unit, 1), cols] = e.sum(0, keepdims=True)
                w_s[pl.ds(unit, 1), cols] = (e * du).sum(0, keepdims=True)
        return carry

    lax.fori_loop(0, nblk, first, 0, unroll=2)

    own = []
    row_in = lax.broadcasted_iota(jnp.int32, (BLK, wide), 1) % BLK
    key_in = lax.broadcasted_iota(jnp.int32, (BLK, wide), 0)
    causal = key_in <= row_in
    for b in range(nb):
        cols = slice(b * wide, (b + 1) * wide)
        bk = bkv_ref[b * BLK:(b + 1) * BLK, :128]
        bv = bkv_ref[b * BLK:(b + 1) * BLK, 128:]
        s = jnp.where(causal, nt(bk, qs[cols, :]) * c, NEG)
        m = s.max(0, keepdims=True)
        e = jnp.exp2(s - m)
        d = nt(bv, dos[cols, :])
        top = jnp.maximum(m, m_s[:, cols].max(0, keepdims=True))
        scales = jnp.exp2(m_s[:, cols] - top)
        mine = jnp.exp2(m - top)
        mass = (l_s[:, cols] * scales).sum(0, keepdims=True) + e.sum(0, keepdims=True) * mine
        dots = (w_s[:, cols] * scales).sum(0, keepdims=True) + (e * d).sum(0, keepdims=True) * mine
        inv = 1.0 / mass
        delta = dots * inv
        f_s[:units, cols] = scales * inv
        f_s[units:units + 1, cols] = delta
        p = e * (mine * inv)
        ds = (p * (d - delta)).astype(BF16)
        p = p.astype(BF16)
        own_k = mm(ds, qs[cols, :]) * scale
        own_v = mm(p, dos[cols, :])
        bg_ref[b * BLK:(b + 1) * BLK, :128] = own_k.astype(BF16)
        bg_ref[b * BLK:(b + 1) * BLK, 128:] = own_v.astype(BF16)
        own.append((own_k.sum(0, keepdims=True), own_v.sum(0, keepdims=True)))
        acc[:, cols] = mm(turn(bk), ds)

    delta = f_s[units:units + 1, :]

    def second(blk, carry):
        sum_k, sum_v = carry
        at = pl.multiple_of(blk * BP, BP)
        p = jnp.concatenate([
            e_s[pl.ds(at + u * KBLK, KBLK), :] * f_s[pl.ds(blk * (BP // KBLK) + u, 1), :]
            for u in range(BP // KBLK)
        ])
        ds = (p * (d_s[pl.ds(at, BP), :] - delta)).astype(BF16)
        p = p.astype(BF16)
        dk = mm(ds, qs[...]) * scale
        dv = mm(p, dos[...])
        acc[...] += mm(turn(kv_s[pl.ds(at, BP), :128]), ds)
        for u in range(0, BP // KBLK, 2):
            to = pl.multiple_of(blk * (BP // 2) + u * (KBLK // 2), KBLK)
            for x, cols in ((dk, slice(0, 128)), (dv, slice(128, 256))):
                x0, x1 = x[u * KBLK:(u + 1) * KBLK], x[(u + 1) * KBLK:(u + 2) * KBLK]
                keep_ref[pl.ds(to, KBLK), cols] = jnp.where(even, x0, x1)
                send_ref[pl.ds(to, KBLK), cols] = jnp.where(even, x1, x0).astype(BF16)
        return (sum_k + dk.sum(0, keepdims=True), sum_v + dv.sum(0, keepdims=True))

    start = (sum(o[0] for o in own), sum(o[1] for o in own))
    sum_k, sum_v = lax.fori_loop(0, nblk, second, start, unroll=2)
    parts = []
    dq = acc[...].T * scale
    for h in range(heads):
        part = jnp.zeros((1, 128), F32)
        for b in range(nb):
            at = (b * heads + h) * BLK
            piece = dq[at:at + BLK, :]
            part += piece.sum(0, keepdims=True)
            dq_ref[b * BLK:(b + 1) * BLK, h * 128:(h + 1) * 128] = piece.astype(BF16)
        parts.append(part)
    parts += [sum_k, sum_v, jnp.zeros((14 - heads, 128), F32)]
    bias_ref[...] = jnp.broadcast_to(jnp.concatenate(parts)[None], bias_ref.shape)


def grads(info, q, do, bkv, near, far, copies):
    rows, width = q.shape
    total = near.shape[0] + far.shape[0]
    wide = rows * width // 128
    units = total // KBLK
    vmem = pl.BlockSpec(memory_space=pltpu.VMEM)
    return pl.pallas_call(
        grads_kernel,
        out_shape=(
            jax.ShapeDtypeStruct((rows, width), BF16),
            jax.ShapeDtypeStruct((rows, 256), BF16),
            jax.ShapeDtypeStruct((total // 2, 256), BF16),
            jax.ShapeDtypeStruct((total // 2, 256), F32),
            jax.ShapeDtypeStruct((copies, 16, 128), F32),
        ),
        in_specs=[pl.BlockSpec(memory_space=pltpu.SMEM)] + [vmem] * 5,
        out_specs=(vmem,) * 5,
        scratch_shapes=[
            pltpu.VMEM((wide, 128), BF16),
            pltpu.VMEM((wide, 128), BF16),
            pltpu.VMEM((total, wide), F32),
            pltpu.VMEM((total, wide), F32),
            pltpu.VMEM((units, wide), F32),
            pltpu.VMEM((units, wide), F32),
            pltpu.VMEM((units, wide), F32),
            pltpu.VMEM((units + 8, wide), F32),
            pltpu.VMEM((128, wide), F32),
            pltpu.VMEM((total, 256), BF16),
        ],
        compiler_params=pltpu.CompilerParams(vmem_limit_bytes=40 * 2**20),
        cost_estimate=pl.CostEstimate(
            flops=10 * wide * total * 128, bytes_accessed=3 * 2**20, transcendentals=wide * total
        ),
    )(info, q, do, bkv, near, far)


SWAP = [(0, 1), (1, 0)]


def body(prompt_kv, queries, branch_kv, dout, prefix):
    n = lax.axis_size("zh")
    zh, zm, zl = (lax.axis_index(a) for a in CTX)
    rows = queries.shape[1]
    nb = rows // BLK
    keys = prompt_kv.shape[1]
    mine = prompt_kv[0]
    column = lax.all_gather(mine, "zh")
    mine, column = lax.optimization_barrier((mine, column))
    near = lax.all_to_all(jnp.broadcast_to(mine[None], (4, keys, 256)), QUAD, 0, 0, tiled=True)
    others = lax.dynamic_slice_in_dim(jnp.concatenate([column, column]), zh + 1, n - 1)
    far = lax.all_gather(others.reshape(-1, 256), QUAD, axis=0, tiled=True)
    mine_prefix = lax.dynamic_slice_in_dim(prefix[0], lax.axis_index(CTX) * nb, nb)
    info = jnp.concatenate([mine_prefix, jnp.stack([zl, zh])])
    dq, bg, send, keep, bias = grads(
        info, queries[0], dout[0], branch_kv[0], near.reshape(-1, 256), far, lax.axis_size(DP)
    )
    got = lax.ppermute(send, "zl", SWAP)
    bias = lax.all_to_all(bias, DP, 0, 0, tiled=True)
    pair = (keep + got.astype(F32)).reshape(n, 2, keys, 256)
    away = lax.dynamic_index_in_dim(pair, 1 - zm, 1, keepdims=False).astype(BF16)
    home = lax.dynamic_index_in_dim(pair, zm, 1, keepdims=False)
    got = lax.ppermute(away, "zm", SWAP)
    bias, away = lax.optimization_barrier((bias, away))
    bias = bias.sum(0)
    bias = lax.psum(bias, QUAD)
    high = bias.astype(BF16)
    low = (bias - high.astype(F32)).astype(BF16)
    extra = jnp.concatenate([high, low], 1)
    parcel = home + got.astype(F32)
    sums = lax.dynamic_index_in_dim(parcel, zh, 0, keepdims=False)
    both = jnp.zeros((16, 256), F32)
    for far in ORDER:
        sent = lax.dynamic_index_in_dim(parcel, (zh + far) % n, 0, keepdims=False)
        sent = jnp.concatenate([sent.astype(BF16), extra])
        came = lax.ppermute(sent, "zh", [(p, (p + far) % n) for p in range(n)]).astype(F32)
        sums += came[:keys]
        both += came[keys:]
    bias = (bias + both[:, :128] + both[:, 128:])[:10].reshape(-1)
    return dq[None], sums[None].astype(BF16), bg[None], bias


def solution(mesh):
    fine = Mesh(
        mesh.devices.reshape(4, 4, 2, mesh.shape["ctx"] // 4, 2, 2),
        ("x", "y", "c", "zh", "zm", "zl"),
    )
    split = P(DP, CTX, None)
    return jax.shard_map(
        body,
        mesh=fine,
        in_specs=(split, split, split, split, P(DP, None)),
        out_specs=(split, split, split, P()),
        check_vma=False,
    )
```
